512 devices in a mesh: ctx: 64 (over y_lo, z, core), tp: 8 (over y_hi, x).
Axes of the slice: x: 4, y: 8 (y_hi: 2, y_lo: 4; y = y_hi * 4 + y_lo), z: 8, core: 2. Of those that a mesh axis runs over, the one named last changes fastest.
Arguments:
- vision_rows: bfloat16 [64, 160, 3584], P('ctx', None, 'tp'), may hold values from -10 to 10
- audio_rows: bfloat16 [64, 64, 1280], P('ctx'), may hold values from -6 to 6
- vision_count: int32 [64], replicated, may hold values from 1 to 160, 6144 in all
- audio_count: int32 [64], replicated, may hold values from 1 to 64, 2048 in all
- position_ids: int32 [3, 64, 224], P(None, 'ctx'), may hold values from 0 to 14335
- audio_proj: bfloat16 [1280, 3584], P(None, 'tp'), may hold values from -0.15625 to 0.15625
- norm_gain: float32 [3584], replicated, may hold values from 0.1 to 1.9
- q_weight: bfloat16 [3584, 2048], P(None, 'tp'), may hold values from -1 to 1
- key_value_weight: bfloat16 [3584, 512], P('tp'), may hold values from -1 to 1
Outputs:
- attended: bfloat16 [64, 224, 2048], P('ctx', None, 'tp')
The draws below stay inside these ranges and needn't reach their ends.
Inputs may be any that keep to these rules, and one draw needn't show every extreme that they name: `vision_count`: sum to 6144, the largest is exactly 160. `audio_count`: sum to 2048, the largest is exactly 64.
All inputs are finite; a program needn't handle non-finite values.
Results may differ from the reference program's by a relative error of at most 0.017.
Values may be sent and summed in bfloat16 or wider, within the bound.
A program may use at most 64 MiB of HBM per device.

```python
import math
import jax
import jax.numpy as jnp
import numpy as np
from jax import lax

D = 3584
AW = 1280
HEAD_WIDTH = 128
QUERY_HEADS = 16
KEY_VALUE_HEADS = 2
VCAP = 160
ACAP = 64
STRETCH_COUNT = 64
STRETCH_TOKENS = 224


def draw_vision_rows(key, part):
    key = jax.random.fold_in(key, 3)
    noise_key = jax.random.fold_in(key, 0)
    rows = jax.random.truncated_normal(noise_key, -6.0, 6.0, (STRETCH_COUNT, VCAP, D), jnp.float32)
    return rows.astype(jnp.bfloat16)


def draw_q_weight(key, part):
    key = jax.random.fold_in(key, 5)
    row_width = QUERY_HEADS * HEAD_WIDTH
    base = jax.random.truncated_normal(key, -6.0, 6.0, (D, row_width), jnp.float32) / math.sqrt(D)
    return base.astype(jnp.bfloat16)


def draw_key_value_weight(key, part):
    key = jax.random.fold_in(key, 7)
    row_width = 2 * KEY_VALUE_HEADS * HEAD_WIDTH
    base = jax.random.truncated_normal(key, -6.0, 6.0, (D, row_width), jnp.float32) / math.sqrt(D)
    return base.astype(jnp.bfloat16)


def plant(values, stream_key, least, high):
    longest = values.shape.index(max(values.shape))
    spots = []
    for shift in (0, 1):
        where = [jax.random.randint(jax.random.fold_in(stream_key, axis), (), 0, length) for axis, length in enumerate(values.shape)]
        where[longest] = (where[longest] + shift) % values.shape[longest]
        spots.append(tuple(where))
    return values.at[spots[0]].set(least).at[spots[1]].set(high)


def level_of(rng, shape, cuts, least, largest):
    level, own = 1.0, jax.random.fold_in(rng, 6)
    for position, parts in cuts:
        draws = jnp.exp(jax.random.uniform(jax.random.fold_in(own, position), (parts,), jnp.float32, least / len(cuts), largest / len(cuts)))
        level = level * jnp.repeat(draws, shape[position] // parts).reshape([-1 if axis == position else 1 for axis in range(len(shape))])
    return level


def length_profile(amount, total, bound, lean):
    portions = [(1 << 20) // math.isqrt(rank ** lean) + 1 for rank in range(2, amount + 1)]
    rest, counts = total - bound - (amount - 1), [1] * (amount - 1)
    while rest > 0:
        free = [i for i in range(amount - 1) if counts[i] < bound]
        whole, remaining = sum([portions[i] for i in free]), rest
        for i in free:
            more = min(bound - counts[i], max(1, remaining * portions[i] // whole), rest)
            counts[i] = counts[i] + more
            rest = rest - more
    return np.array([bound] + counts)


def ragged_sizes(key, amount, total, bound, lean):
    if amount == 2:
        one = jax.random.randint(key, (), max(1, total - bound), min(bound, total - 1) + 1)
        return jnp.stack([one, total - one])
    lengths = jnp.asarray(length_profile(amount, total, bound, lean), jnp.int32)
    couples = (amount - 1) // 2
    donor, taker = lengths[1:1 + 2 * couples:2], lengths[2:2 + 2 * couples:2]
    margin = jnp.minimum(donor - 1, bound - taker)
    moved = jax.random.randint(jax.random.fold_in(key, 1), (couples,), 0, 1 << 20) % (margin + 1)
    lengths = lengths.at[1:1 + 2 * couples:2].set(donor - moved).at[2:2 + 2 * couples:2].set(taker + moved)
    return lengths[jax.random.permutation(jax.random.fold_in(key, 2), amount)]


def gaussian(stream_key, dims, spread, most, cuts=(), kind=jnp.bfloat16):
    values = spread * jax.random.normal(stream_key, dims, jnp.float32)
    if cuts:
        values = values * level_of(stream_key, dims, cuts, -0.22, 0.18)
    return jnp.clip(values, -most, most).astype(kind)


def setup_inputs(seed: int = 0) -> dict:
    streams_of = jax.random.split(jax.random.key(seed), 10)
    return {
        "vision_rows": draw_vision_rows(jax.random.fold_in(streams_of[9], 71), 0),
        "audio_rows": gaussian(streams_of[1], (STRETCH_COUNT, ACAP, AW), 1.0, 6.0, ((0, 64),)),
        "vision_count": ragged_sizes(streams_of[2], STRETCH_COUNT, VCAP * 3 // 5 * STRETCH_COUNT, VCAP, 2).astype(jnp.int32),
        "audio_count": ragged_sizes(streams_of[3], STRETCH_COUNT, ACAP // 2 * STRETCH_COUNT, ACAP, 1).astype(jnp.int32),
        "position_ids": plant(jax.random.randint(streams_of[4], (3, STRETCH_COUNT, STRETCH_TOKENS), 0, STRETCH_COUNT * STRETCH_TOKENS), jax.random.fold_in(streams_of[4], 1), 0, (STRETCH_COUNT * STRETCH_TOKENS) - 1).astype(jnp.int32),
        "audio_proj": gaussian(streams_of[5], (AW, D), AW ** -0.5, 0.15625, ((1, 8),)),
        "norm_gain": jnp.clip(1.0 + 0.18 * jax.random.normal(streams_of[6], (D,), jnp.float32), 0.1, 1.9),
        "q_weight": draw_q_weight(jax.random.fold_in(streams_of[9], 71), 0),
        "key_value_weight": draw_key_value_weight(jax.random.fold_in(streams_of[9], 71), 0),
    }


def section_index(half_size):
    first = half_size // 4
    second = (half_size - first) // 2
    return np.array([0] * first + [1] * second + [2] * (half_size - first - second), dtype=np.int32)

def rope_tables(position_ids, head_size):
    half_size = head_size // 2
    chosen = position_ids[section_index(half_size)].astype(jnp.float32)
    chosen = jnp.moveaxis(chosen, 0, -1)
    inverse = jnp.exp(-math.log(1000000.0) * 2.0 * jnp.arange(half_size, dtype=jnp.float32) / head_size)
    angle_table = chosen * inverse
    return (jnp.cos(angle_table), jnp.sin(angle_table))

def rotate(values_in, cosine_table, sine_table):
    half_size = values_in.shape[-1] // 2
    first = values_in[..., :half_size]
    second = values_in[..., half_size:]
    cosine_b = cosine_table[..., None, :]
    sine_b = sine_table[..., None, :]
    return jnp.concatenate([first * cosine_b - second * sine_b, second * cosine_b + first * sine_b], axis=-1)

def reference(vision_rows, audio_rows, vision_count, audio_count, position_ids, audio_proj, norm_gain, q_weight, key_value_weight):
    audio_hidden = jnp.dot(audio_rows.reshape(-1, AW), audio_proj, preferred_element_type=jnp.float32)
    audio_hidden = audio_hidden.astype(jnp.bfloat16).reshape(STRETCH_COUNT, ACAP, D)
    stacked = jnp.concatenate([vision_rows, audio_hidden], axis=1)
    slot_rows = jnp.arange(STRETCH_TOKENS, dtype=jnp.int32)[None, :]
    vision_here = vision_count.astype(jnp.int32)[:, None]
    totals = (vision_count + audio_count).astype(jnp.int32)
    slot_live = slot_rows < totals[:, None]
    source_index = jnp.where(slot_rows < vision_here, slot_rows, VCAP + slot_rows - vision_here)
    source_index = jnp.clip(source_index, 0, STRETCH_TOKENS - 1).astype(jnp.int32)
    embedded = jnp.take_along_axis(stacked, source_index[..., None], axis=1)
    embedded = jnp.where(slot_live[..., None], embedded, jnp.zeros_like(embedded))
    feature_f32 = embedded.astype(jnp.float32)
    mean_square = lax.optimization_barrier(jnp.mean(feature_f32 * feature_f32, axis=-1, keepdims=True))
    normed = (feature_f32 * lax.rsqrt(mean_square + 1e-06) * norm_gain).astype(jnp.bfloat16)
    flattened = normed.reshape(-1, D)
    cosine_table, sine_table = rope_tables(position_ids, HEAD_WIDTH)
    queries = jnp.dot(flattened, q_weight, preferred_element_type=jnp.float32).reshape(STRETCH_COUNT, STRETCH_TOKENS, QUERY_HEADS, HEAD_WIDTH)
    queries = rotate(queries, cosine_table, sine_table).astype(jnp.bfloat16)
    key_value_full = jnp.dot(flattened, key_value_weight, preferred_element_type=jnp.float32).reshape(STRETCH_COUNT, STRETCH_TOKENS, 2, KEY_VALUE_HEADS, HEAD_WIDTH)
    key_rows = rotate(key_value_full[:, :, 0], cosine_table, sine_table).astype(jnp.bfloat16)
    value_rows = key_value_full[:, :, 1].astype(jnp.bfloat16)
    starts = (jnp.cumsum(totals) - totals).astype(jnp.int32)
    seq_pos = starts[:, None] + slot_rows
    key_pos = seq_pos.reshape(-1)
    key_live = slot_live.reshape(-1)
    key_rows_float = key_rows.reshape(-1, KEY_VALUE_HEADS, HEAD_WIDTH).astype(jnp.float32)
    value_rows_float = value_rows.reshape(-1, KEY_VALUE_HEADS, HEAD_WIDTH).astype(jnp.float32)
    head_group = QUERY_HEADS // KEY_VALUE_HEADS
    scale = HEAD_WIDTH ** (-0.5)

    def one_stretch(inputs):
        query_tile_rows, query_pos, query_live = inputs
        heads_of_query = query_tile_rows.astype(jnp.float32).reshape(STRETCH_TOKENS, KEY_VALUE_HEADS, head_group, HEAD_WIDTH)
        scores = jnp.einsum('qhgd,khd->hgqk', heads_of_query, key_rows_float, precision=lax.Precision.HIGHEST) * scale
        counted = (key_pos[None, :] <= query_pos[:, None]) & key_live[None, :]
        scores = jnp.where(counted, scores, -1e+30)
        row_max = lax.optimization_barrier(jnp.max(scores, axis=-1, keepdims=True))
        weights = jnp.where(counted, jnp.exp(scores - row_max), 0.0)
        weight_sum = lax.optimization_barrier(jnp.sum(weights, axis=-1))
        rounded = lax.optimization_barrier(weights.astype(jnp.bfloat16)).astype(jnp.float32)
        summed = jnp.einsum('hgqk,khd->qhgd', rounded, value_rows_float, precision=lax.Precision.HIGHEST)
        denom = jnp.where(query_live[:, None, None], jnp.transpose(weight_sum, (2, 0, 1)), 1.0)
        result = jnp.where(query_live[:, None, None, None], summed / denom[..., None], 0.0)
        return result.reshape(STRETCH_TOKENS, QUERY_HEADS * HEAD_WIDTH).astype(jnp.bfloat16)
    return lax.map(one_stretch, (queries, seq_pos, slot_live))
```

```python
import functools
import math

import jax
import jax.numpy as jnp
import numpy as np
from jax import lax
from jax.experimental import pallas as pl
from jax.experimental.pallas import tpu as pltpu
from jax.sharding import PartitionSpec as P

HW = 128
MESH = pl.DeviceIdType.MESH
F32 = jnp.float32
BF16 = jnp.bfloat16

NY, NZ, NC, NX = 4, 8, 2, 4
VC, AC, T = 160, 64, 224
DS, D = 448, 3584
CH = 64
LIVE_CH = T // NX
HALF = T // 2
KB = 512
NEG = -1e30
QSCALE = HW**-0.5 * math.log2(math.e)


def iota(shape, dim):
    return lax.broadcasted_iota(jnp.int32, shape, dim)


def place():
    ctx, tp = lax.axis_index("ctx"), lax.axis_index("tp")
    return dict(yl=ctx // (NZ * NC), z=(ctx // NC) % NZ, core=ctx % NC, h=tp // NX, x=tp % NX, ctx=ctx, tp=tp)


def device(at, yl=None, z=None, core=None, h=None, x=None):
    yl = at["yl"] if yl is None else yl
    z = at["z"] if z is None else z
    core = at["core"] if core is None else core
    h = at["h"] if h is None else h
    x = at["x"] if x is None else x
    return ((yl * NZ + z) * NC + core, h * NX + x)


def along_y(at, by):
    y = (at["h"] * NY + at["yl"] + by) % (2 * NY)
    return device(at, h=y // NY, yl=y % NY)


def swap_halves(a):
    return jnp.concatenate([a[:, HW // 2 :], a[:, : HW // 2]], axis=1)


def rope(a, cos, sin):
    return a * cos + swap_halves(a) * sin


def tables(pos_ref, inv_ref, pick):
    rows = pick.shape[0]
    ids = [
        jnp.sum(jnp.where(pick, pos_ref[k].astype(F32), 0.0), axis=1, keepdims=True) for k in range(3)
    ]
    lane = iota((rows, HW), 1)
    freq = lane % (HW // 2)
    first = HW // 8
    second = (HW // 2 - first) // 2
    chosen = jnp.where(freq < first, ids[0], jnp.where(freq < first + second, ids[1], ids[2]))
    angle = chosen * inv_ref[...]
    sin = jnp.sin(angle)
    return jnp.cos(angle), jnp.where(lane < HW // 2, -sin, sin)


def gather_kernel(
    vcount, acount, pos_ref, inv_ref, gain_ref, vision_ref, audio_ref, proj_ref, kvw_ref, qw_hbm,
    q_out, kv_out,
    stacked, feat, via, part, rsbuf, qw, qw_sem, ssem, rsem,
):
    at = place()
    ctx, tp, x, h = at["ctx"], at["tp"], at["x"], at["h"]
    fetch = pltpu.make_async_copy(qw_hbm, qw, qw_sem)
    fetch.start()

    right = device(at, x=(x + 1) % NX)
    left = device(at, x=(x + 3) % NX)
    up = device(at, z=(at["z"] + 1) % NZ)
    down = device(at, z=(at["z"] + 7) % NZ)
    sibling = device(at, core=1 - at["core"])
    y_plus, y_minus = along_y(at, 2), along_y(at, 6)
    tp_peers = [(ctx, (tp + e) % 8) for e in range(1, 8)]
    y_peers = [device(at, yl=(at["yl"] + e) % NY) for e in range(1, NY)]
    greeted = [up, down, sibling, y_plus, y_minus] + tp_peers + y_peers
    barrier = pltpu.get_barrier_semaphore()
    for other in greeted:
        pl.semaphore_signal(barrier, inc=1, device_id=other, device_id_type=MESH)

    copies = []

    def remote(src, dst, to):
        i = len(copies)
        copy = pltpu.make_async_remote_copy(
            src_ref=src, dst_ref=dst, send_sem=ssem.at[i], recv_sem=rsem.at[i], device_id=to, device_id_type=MESH
        )
        copies.append(copy)
        copy.start()
        return copy

    vision_here = vcount[ctx]
    total = vision_here + acount[ctx]
    stacked[:VC] = vision_ref[0]
    stacked[VC:] = jnp.dot(audio_ref[0], proj_ref[...], preferred_element_type=F32).astype(BF16)

    def picked(slot, valid):
        source = jnp.where(slot < vision_here, slot, VC + slot - vision_here)
        hit = (iota((slot.shape[0], T), 1) == source) & (slot < total) & valid
        onehot = jnp.where(hit, 1.0, 0.0).astype(BF16)
        return jnp.dot(onehot, stacked[...], preferred_element_type=F32)

    slot = iota((T, 1), 0)
    feat[0, 0] = picked(slot, slot >= 0).astype(BF16)
    pl.semaphore_wait(barrier, len(greeted))

    top, low = pl.ds(0, HALF), pl.ds(HALF, HALF)
    via_plus = remote(feat.at[0, 0, top], via.at[0], y_plus)
    via_minus = remote(feat.at[0, 0, low], via.at[1], y_minus)
    from_left = [remote(feat.at[0, 0], feat.at[0, 3], right), None]
    from_right = [remote(feat.at[0, 0], feat.at[0, 1], left), None]

    row = iota((NX * CH, 1), 0)
    chunk_row = row % CH
    chunked = picked(chunk_row * NX + row // CH, chunk_row < LIVE_CH)
    squares = jnp.sum(chunked * chunked, axis=1, keepdims=True)
    gained = (chunked * gain_ref[pl.ds(tp, 1)]).astype(BF16)
    term = jnp.dot(gained, kvw_ref[...], preferred_element_type=F32)
    crow, clane = iota((CH, 2 * HW), 0), iota((CH, 2 * HW), 1)
    for g in range(2):
        for j in range(NX):
            rows = slice(j * CH, (j + 1) * CH)
            keys = term[rows, g * HW : (g + 1) * HW]
            values = term[rows, (2 + g) * HW : (3 + g) * HW]
            line = jnp.sum(jnp.where(crow == clane, squares[rows], 0.0), axis=0, keepdims=True)
            high = line.astype(BF16).astype(F32)
            block = jnp.concatenate([keys, values], axis=1)
            block = jnp.where(crow == LIVE_CH, high, jnp.where(crow == LIVE_CH + 1, line - high, block))
            part[g * NX + j] = block.astype(BF16)
    terms = [remote(part.at[(tp + e) % 8], rsbuf.at[8 - e], tp_peers[e - 1]) for e in range(1, 8)]

    pick = iota((CH, T), 1) == iota((CH, T), 0) * NX + x
    cos_k, sin_k = tables(pos_ref, inv_ref, pick)

    via_plus.wait_recv()
    partner_top = remote(via.at[0], feat.at[1, 0, top], y_plus)
    via_minus.wait_recv()
    partner_low = remote(via.at[1], feat.at[1, 0, low], y_minus)

    summed = part[tp].astype(F32)
    for e in range(1, 8):
        terms[e - 1].wait_recv()
        summed = summed + rsbuf[8 - e].astype(F32)
    line = summed[LIVE_CH : LIVE_CH + 1] + summed[LIVE_CH + 1 : LIVE_CH + 2]
    squares = jnp.sum(jnp.where(crow == clane, line, 0.0), axis=1, keepdims=True)
    scaled = summed * lax.rsqrt(squares / D + 1e-06)
    live = (iota((CH, HW), 0) * NX + x < total) & (iota((CH, HW), 0) < LIVE_CH)
    keys = rope(scaled[:, :HW], cos_k, sin_k)
    keys = jnp.where(live, keys, keys[0:1])
    values = jnp.where(live, scaled[:, HW:], 0.0)
    kv_out[0, 0, 0] = jnp.concatenate([keys, values], axis=1).astype(BF16)

    y_moves = [remote(kv_out.at[0, 0, 0], kv_out.at[0, 0, NY - e], y_peers[e - 1]) for e in range(1, NY)]
    ups, downs = {}, {}

    def send_up(t, dy):
        ups[t, dy] = remote(kv_out.at[-t % NZ, 0, dy], kv_out.at[(-t - 1) % NZ, 0, dy], up)

    def send_down(t, dy):
        downs[t, dy] = remote(kv_out.at[t, 0, dy], kv_out.at[t + 1, 0, dy], down)

    send_up(0, 0)
    send_down(0, 0)

    def pass_on(g):
        from_left[g].wait_recv()
        a = remote(feat.at[g, 3, top], feat.at[g, 2, top], right)
        from_right[g].wait_recv()
        b = remote(feat.at[g, 1, low], feat.at[g, 2, low], left)
        return a, b

    far = [pass_on(0), None]
    partner_top.wait_recv()
    partner_low.wait_recv()
    from_left[1] = remote(feat.at[1, 0], feat.at[1, 3], right)
    from_right[1] = remote(feat.at[1, 0], feat.at[1, 1], left)
    for e in range(1, NY):
        y_moves[e - 1].wait_recv()
        send_up(0, NY - e)
        send_down(0, NY - e)
    siblings = [remote(kv_out.at[0, 0], kv_out.at[0, 1], sibling)]

    fetch.wait()
    pick = iota((T, T), 1) == iota((T, T), 0)
    cos_q, sin_q = tables(pos_ref, inv_ref, pick)
    acc = [jnp.zeros((T, 2 * HW), F32), jnp.zeros((T, 1), F32)]

    def add(g, d):
        piece = ((h + g) % 2) * NX + (x + d) % NX
        wide = feat[g, d].astype(F32)
        acc[1] = acc[1] + jnp.sum(wide * wide, axis=1, keepdims=True)
        gained = (wide * gain_ref[pl.ds(piece, 1)]).astype(BF16)
        acc[0] = acc[0] + jnp.dot(gained, qw[pl.ds(pl.multiple_of(piece * DS, DS), DS)], preferred_element_type=F32)

    def z_step(t):
        for dy in range(NY):
            ups[t - 1, dy].wait_recv()
            if t < 3 or dy < 2:
                send_up(t, dy)
            downs[t - 1, dy].wait_recv()
            if t < 3 or dy >= 2:
                send_down(t, dy)
        siblings.append(remote(kv_out.at[NZ - t, 0], kv_out.at[NZ - t, 1], sibling))
        siblings.append(remote(kv_out.at[t, 0], kv_out.at[t, 1], sibling))

    add(0, 0)
    z_step(1)
    add(0, 3)
    add(0, 1)
    far[0][0].wait_recv()
    far[0][1].wait_recv()
    far[1] = pass_on(1)
    add(0, 2)
    add(1, 0)
    z_step(2)
    add(1, 3)
    add(1, 1)
    z_step(3)
    far[1][0].wait_recv()
    far[1][1].wait_recv()
    add(1, 2)
    queries = acc[0] * (lax.rsqrt(acc[1] / D + 1e-06) * QSCALE)
    q_out[0] = jnp.concatenate(
        [rope(queries[:, :HW], cos_q, sin_q), rope(queries[:, HW:], cos_q, sin_q)], axis=1
    ).astype(BF16)
    q_moves = [
        remote(q_out.at[0], q_out.at[NX - e], device(at, x=(x + e) % NX)) for e in range(1, NX)
    ]
    for dy in range(NY):
        (ups if dy < 2 else downs)[3, dy].wait_recv()
    siblings.append(remote(kv_out.at[4, 0], kv_out.at[4, 1], sibling))
    for copy in siblings + q_moves:
        copy.wait_recv()
    for copy in copies:
        copy.wait_send()


COPIES = 2 + 2 + 2 + 2 + 4 + 2 + 7 + 3 + 28 + 8 + 3


def attend_kernel(
    vcount, acount, q_ref, kv_ref, o_ref, stat_ref, kc, vc, vown, m_ref, acc_ref
):
    at = place()
    ctx, x = at["ctx"], at["x"]

    def live_rows(s):
        return (vcount[s] + acount[s] - x + NX - 1) // NX

    crow = iota((CH, HW), 0)

    def compact(j, off):
        dz, dc, dy = j // (NC * NY), (j // NY) % NC, j % NY
        s = (((at["yl"] + dy) % NY) * NZ + (at["z"] + dz) % NZ) * NC + (at["core"] + dc) % NC
        rows = live_rows(s)
        block = kv_ref[dz, dc, dy]
        where = pl.ds(pl.multiple_of(off, 16), CH)
        kc[where] = block[:, :HW]
        vc[where, :HW] = block[:, HW:]
        vc[where, HW:] = jnp.where(crow < rows, 1.0, 0.0).astype(BF16)
        return off + jnp.where(s < ctx, ((rows + 15) // 16) * 16, 0)

    count = lax.fori_loop(0, NZ * NC * NY, compact, jnp.int32(0))
    tail = pl.ds(pl.multiple_of(count, 16), KB)
    kc[tail] = jnp.broadcast_to(kc[0:1], (KB, HW))
    vc[tail] = jnp.zeros((KB, 2 * HW), BF16)

    own = kv_ref[0, 0, 0]
    own_rows = live_rows(ctx)
    vown[:, :HW] = own[:, HW:]
    vown[:, HW:] = jnp.where(crow < own_rows, 1.0, 0.0).astype(BF16)
    key = iota((T, CH), 1)
    counted = (key * NX + x <= iota((T, CH), 0)) & (key < own_rows)
    nt = (((1,), (1,)), ((), ()))
    blocks = [(j, k) for j in range(NX) for k in range(2)]
    for b, (j, k) in enumerate(blocks):
        q = q_ref[j, :, k * HW : (k + 1) * HW]
        s = lax.dot_general(q, own[:, :HW], nt, preferred_element_type=F32)
        s = jnp.where(counted, s, NEG)
        m = jnp.max(s, axis=1, keepdims=True)
        p = jnp.where(counted, jnp.exp2(s - m), 0.0).astype(BF16)
        m_ref[b] = m
        acc_ref[b] = jnp.dot(p, vown[...], preferred_element_type=F32)

    def step(i, carry):
        rows = pl.ds(pl.multiple_of(i * KB, KB), KB)
        for b, (j, k) in enumerate(blocks):
            q = q_ref[j, :, k * HW : (k + 1) * HW]
            s = lax.dot_general(q, kc[rows], nt, preferred_element_type=F32)
            before = m_ref[b]
            m = jnp.maximum(before, jnp.max(s, axis=1, keepdims=True))
            p = jnp.exp2(s - m).astype(BF16)
            m_ref[b] = m
            acc_ref[b] = acc_ref[b] * jnp.exp2(before - m) + jnp.dot(p, vc[rows], preferred_element_type=F32)
        return carry

    lax.fori_loop(0, (count + KB - 1) // KB, step, 0)

    eye = iota((T, T), 0) == iota((T, T), 1)
    stat_ref[...] = jnp.zeros_like(stat_ref)
    for b, (j, k) in enumerate(blocks):
        acc = acc_ref[b]
        total = acc[:, HW : HW + 1]
        some = total > 0.0
        safe = jnp.where(some, total, 1.0)
        o_ref[j, :, k * HW : (k + 1) * HW] = (acc[:, :HW] / safe).astype(BF16)
        level = jnp.where(some, m_ref[b] + jnp.log2(safe), NEG)
        stat_ref[j, k : k + 1, :T] = jnp.sum(jnp.where(eye, level, 0.0), axis=0, keepdims=True)


def combine_kernel(vcount, acount, o_ref, stat_ref, out_ref, obuf, sbuf, ssem, rsem):
    at = place()
    ctx, x = at["ctx"], at["x"]
    peers = [device(at, x=(x + e) % NX) for e in range(1, NX)]
    barrier = pltpu.get_barrier_semaphore()
    for other in peers:
        pl.semaphore_signal(barrier, inc=1, device_id=other, device_id_type=MESH)
    pl.semaphore_wait(barrier, len(peers))
    copies = []
    for e in range(1, NX):
        for n, (src, dst) in enumerate([(o_ref, obuf), (stat_ref, sbuf)]):
            copy = pltpu.make_async_remote_copy(
                src_ref=src.at[e], dst_ref=dst.at[NX - e], send_sem=ssem.at[n, e], recv_sem=rsem.at[n, e],
                device_id=peers[e - 1], device_id_type=MESH,
            )
            copy.start()
            copies.append(copy)
    eye = iota((T, T), 0) == iota((T, T), 1)

    def column(line):
        return jnp.sum(jnp.where(eye, line[:, :T], 0.0), axis=1, keepdims=True)

    for copy in copies:
        copy.wait_recv()
    live = iota((T, HW), 0) < vcount[ctx] + acount[ctx]
    for k in range(2):
        cols = slice(k * HW, (k + 1) * HW)
        levels = [column((stat_ref if j == 0 else sbuf)[j, k : k + 1]) for j in range(NX)]
        peak = functools.reduce(jnp.maximum, levels)
        shares = [jnp.exp2(level - peak) for level in levels]
        parts = [(o_ref if j == 0 else obuf)[j, :, cols].astype(F32) for j in range(NX)]
        summed = sum(s * a for s, a in zip(shares, parts))
        out_ref[0, :, cols] = jnp.where(live, summed / sum(shares), 0.0).astype(BF16)
    for copy in copies:
        copy.wait_send()


def whole():
    return pl.BlockSpec(memory_space=pltpu.VMEM)


def scalars():
    return pl.BlockSpec(memory_space=pltpu.SMEM)


LIMIT = 48 * 1024 * 1024


def per_device(
    vision_rows, audio_rows, vision_count, audio_count, position_ids, audio_proj, norm_gain, q_weight, key_value_weight
):
    lane = np.arange(HW) % (HW // 2)
    inverse = np.exp(-math.log(1000000.0) * 2.0 * lane / HW).astype(np.float32)[None]
    q_all, kv_all = pl.pallas_call(
        gather_kernel,
        out_shape=(
            jax.ShapeDtypeStruct((NX, T, 2 * HW), BF16),
            jax.ShapeDtypeStruct((NZ, NC, NY, CH, 2 * HW), BF16),
        ),
        in_specs=[scalars(), scalars()] + [whole()] * 7 + [pl.BlockSpec(memory_space=pl.ANY)],
        out_specs=(whole(), whole()),
        scratch_shapes=[
            pltpu.VMEM((T, DS), BF16),
            pltpu.VMEM((2, NX, T, DS), BF16),
            pltpu.VMEM((2, HALF, DS), BF16),
            pltpu.VMEM((8, CH, 2 * HW), BF16),
            pltpu.VMEM((8, CH, 2 * HW), BF16),
            pltpu.VMEM((D, 2 * HW), BF16),
            pltpu.SemaphoreType.DMA,
            pltpu.SemaphoreType.DMA((COPIES,)),
            pltpu.SemaphoreType.DMA((COPIES,)),
        ],
        compiler_params=pltpu.CompilerParams(collective_id=0, has_side_effects=True, vmem_limit_bytes=LIMIT),
        name="gather",
    )(
        vision_count, audio_count, position_ids, jnp.asarray(inverse), norm_gain.reshape(8, DS),
        vision_rows, audio_rows, audio_proj, key_value_weight, q_weight,
    )
    longest = NZ * NC * NY * CH + KB
    o_part, stats = pl.pallas_call(
        attend_kernel,
        out_shape=(
            jax.ShapeDtypeStruct((NX, T, 2 * HW), BF16),
            jax.ShapeDtypeStruct((NX, 8, 256), F32),
        ),
        in_specs=[scalars(), scalars(), whole(), whole()],
        out_specs=(whole(), whole()),
        scratch_shapes=[
            pltpu.VMEM((longest, HW), BF16),
            pltpu.VMEM((longest, 2 * HW), BF16),
            pltpu.VMEM((CH, 2 * HW), BF16),
            pltpu.VMEM((8, T, 1), F32),
            pltpu.VMEM((8, T, 2 * HW), F32),
        ],
        compiler_params=pltpu.CompilerParams(vmem_limit_bytes=LIMIT),
        name="attend",
    )(vision_count, audio_count, q_all, kv_all)
    return pl.pallas_call(
        combine_kernel,
        out_shape=jax.ShapeDtypeStruct((1, T, 2 * HW), BF16),
        in_specs=[scalars(), scalars(), whole(), whole()],
        out_specs=whole(),
        scratch_shapes=[
            pltpu.VMEM((NX, T, 2 * HW), BF16),
            pltpu.VMEM((NX, 8, 256), F32),
            pltpu.SemaphoreType.DMA((2, NX)),
            pltpu.SemaphoreType.DMA((2, NX)),
        ],
        compiler_params=pltpu.CompilerParams(collective_id=1, has_side_effects=True, vmem_limit_bytes=LIMIT),
        name="combine",
    )(vision_count, audio_count, o_part, stats)


def solution(mesh):
    placed = (
        P("ctx", None, "tp"),
        P("ctx", None, None),
        P(),
        P(),
        P(None, "ctx", None),
        P(None, "tp"),
        P(),
        P(None, "tp"),
        P("tp", None),
    )
    return jax.shard_map(
        per_device, mesh=mesh, in_specs=placed, out_specs=P("ctx", None, "tp"), check_vma=False
    )
```

```python
import functools
import math

import jax
import jax.numpy as jnp
import numpy as np
from jax import lax
from jax.experimental import pallas as pl
from jax.experimental.pallas import tpu as pltpu
from jax.sharding import PartitionSpec as P

HW = 128
MESH = pl.DeviceIdType.MESH
F32 = jnp.float32
BF16 = jnp.bfloat16

NY, NZ, NC, NX = 4, 8, 2, 4
VC, AC, T = 160, 64, 224
AW = 1280
DS, D = 448, 3584
CH = 64
LIVE_CH = T // NX
TOP, LOW = pl.ds(0, T // 2), pl.ds(T // 2, T // 2)
PIECES = [pl.ds(0, 64), pl.ds(64, 48), pl.ds(112, 64), pl.ds(176, 48)]
NT = (((1,), (1,)), ((), ()))
MASKED, LEAST = -1e30, -1e29
QSCALE = HW**-0.5 * math.log2(math.e)


def iota(shape, dim):
    return lax.broadcasted_iota(jnp.int32, shape, dim)


def place():
    ctx, tp = lax.axis_index("ctx"), lax.axis_index("tp")
    return dict(yl=ctx // (NZ * NC), z=(ctx // NC) % NZ, core=ctx % NC, h=tp // NX, x=tp % NX, ctx=ctx, tp=tp)


def device(at, yl=None, z=None, core=None, h=None, x=None):
    yl = at["yl"] if yl is None else yl
    z = at["z"] if z is None else z
    core = at["core"] if core is None else core
    h = at["h"] if h is None else h
    x = at["x"] if x is None else x
    return ((yl * NZ + z) * NC + core, h * NX + x)


def swap_halves(a):
    return jnp.concatenate([a[:, HW // 2 :], a[:, : HW // 2]], axis=1)


def rope(a, cos, sin):
    return a * cos + swap_halves(a) * sin


def tables(pos_ref, inv_ref, pick):
    rows = pick.shape[0]
    ids = [
        jnp.sum(jnp.where(pick, pos_ref[k].astype(F32), 0.0), axis=1, keepdims=True) for k in range(3)
    ]
    lane = iota((rows, HW), 1)
    freq = lane % (HW // 2)
    first = HW // 8
    second = (HW // 2 - first) // 2
    chosen = jnp.where(freq < first, ids[0], jnp.where(freq < first + second, ids[1], ids[2]))
    angle = chosen * inv_ref[...]
    sin = jnp.sin(angle)
    return jnp.cos(angle), jnp.where(lane < HW // 2, -sin, sin)


def gain_rows(gain_ref):
    g = gain_ref[...]
    half = HW // 2
    rows = []
    for u in range(4):
        r = [g[7 * u + k : 7 * u + k + 1] for k in range(7)]
        rows.append(jnp.concatenate([r[0], r[1], r[2], r[3][:, :half]], axis=1))
        rows.append(jnp.concatenate([r[3][:, half:], r[4], r[5], r[6]], axis=1))
    return jnp.concatenate(rows, axis=0)


def layer_kernel(
    vcount, acount, pos_hbm, inv_ref, gain_ref, vision_hbm, audio_hbm, proj_hbm, kvw_hbm, qw_hbm,
    out_ref,
    pos_ref, vision_ref, audio_ref, proj_ref, kvw_ref, qw,
    stacked, gains, feat, part, xbuf, ysend, ybuf, q_all, kv, bias, m_ref, acc_ref, o_part, stat, obuf, sbuf,
    fetch_sem, ssem, rsem,
):
    at = place()
    ctx, tp, x, h = at["ctx"], at["tp"], at["x"], at["h"]
    fetches = []
    for src, dst in [
        (audio_hbm, audio_ref), (proj_hbm, proj_ref), (vision_hbm, vision_ref), (kvw_hbm, kvw_ref), (pos_hbm, pos_ref), (qw_hbm, qw)
    ]:
        fetches.append(pltpu.make_async_copy(src, dst, fetch_sem.at[len(fetches)]))
        fetches[-1].start()

    right = device(at, x=(x + 1) % NX)
    left = device(at, x=(x + 3) % NX)
    up = device(at, z=(at["z"] + 1) % NZ)
    down = device(at, z=(at["z"] + 7) % NZ)
    sibling = device(at, core=1 - at["core"])
    partner = device(at, h=1 - h)
    x_peers = [device(at, x=(x + e) % NX) for e in range(1, NX)]
    y_peers = [device(at, yl=(at["yl"] + e) % NY) for e in range(1, NY)]
    greeted = [up, down, sibling, partner] + x_peers + y_peers
    barrier = pltpu.get_barrier_semaphore()
    for other in greeted:
        pl.semaphore_signal(barrier, inc=1, device_id=other, device_id_type=MESH)

    copies = []

    def remote(src, dst, to):
        i = len(copies)
        copy = pltpu.make_async_remote_copy(
            src_ref=src, dst_ref=dst, send_sem=ssem.at[i], recv_sem=rsem.at[i], device_id=to, device_id_type=MESH
        )
        copies.append(copy)
        copy.start()
        return copy

    vision_here = vcount[ctx]
    total = vision_here + acount[ctx]
    fetches[0].wait()
    fetches[1].wait()
    stacked[VC:] = lax.dot_general(audio_ref[0], proj_ref[...], NT, preferred_element_type=F32).astype(BF16)
    fetches[2].wait()
    stacked[:VC] = vision_ref[0]

    def picked(slot, valid):
        source = jnp.where(slot < vision_here, slot, VC + slot - vision_here)
        hit = (iota((slot.shape[0], T), 1) == source) & (slot < total) & valid
        onehot = jnp.where(hit, 1.0, 0.0).astype(BF16)
        return jnp.dot(onehot, stacked[...], preferred_element_type=F32)

    slot = iota((T, 1), 0)
    feat[0, 0] = picked(slot, slot >= 0).astype(BF16)
    pl.semaphore_wait(barrier, len(greeted))
    crossed = {p: remote(feat.at[0, 0, PIECES[p]], feat.at[1, 0, PIECES[p]], partner) for p in (0, 2, 1, 3)}

    row = iota((NX * CH, 1), 0)
    chunk_row = row % CH
    chunked = picked(chunk_row * NX + row // CH, chunk_row < LIVE_CH)
    squares = jnp.sum(chunked * chunked, axis=1, keepdims=True)
    gains[...] = gain_rows(gain_ref)
    gained = (chunked * gains[pl.ds(tp, 1)]).astype(BF16)
    fetches[3].wait()
    term = jnp.dot(gained, kvw_ref[...], preferred_element_type=F32)
    crow, clane = iota((CH, 4 * HW), 0), iota((CH, 4 * HW), 1)
    for j in range(NX):
        rows = slice(j * CH, (j + 1) * CH)
        line = jnp.sum(jnp.where(crow == clane % (2 * HW), squares[rows], 0.0), axis=0, keepdims=True)
        high = line.astype(BF16).astype(F32)
        t = term[rows]
        block = jnp.concatenate(
            [t[:, :HW], t[:, 2 * HW : 3 * HW], t[:, HW : 2 * HW], t[:, 3 * HW :]], axis=1
        )
        block = jnp.where(crow == LIVE_CH, high, jnp.where(crow == LIVE_CH + 1, line - high, block))
        part[j] = block.astype(BF16)
    terms = [remote(part.at[(x + e) % NX], xbuf.at[NX - e], x_peers[e - 1]) for e in (2, 1, 3)]
    from_left = [[remote(feat.at[0, 0], feat.at[0, 3], right)]]
    from_right = [[remote(feat.at[0, 0], feat.at[0, 1], left)]]

    fetches[4].wait()
    pick = iota((CH, T), 1) == iota((CH, T), 0) * NX + x
    cos_k, sin_k = tables(pos_ref, inv_ref, pick)

    dz, lane = iota((NZ, NC * NY * CH), 0), iota((NZ, NC * NY * CH), 1)
    dc, dy, i = lane // (NY * CH), (lane // CH) % NY, lane % CH
    stretch = (((at["yl"] + dy) % NY) * NZ + (at["z"] + dz) % NZ) * NC + (at["core"] + dc) % NC
    lengths = jnp.zeros_like(stretch)
    for k in range(NY * NZ * NC):
        lengths = jnp.where(stretch == k, vcount[k] + acount[k], lengths)
    counted = (stretch < ctx) & (i < LIVE_CH) & (i * NX + x < lengths)
    bias[...] = jnp.where(counted, 0.0, MASKED)

    summed = part[x].astype(F32)
    for copy, e in zip(terms, (2, 1, 3)):
        copy.wait_recv()
        summed = summed + xbuf[NX - e].astype(F32)
    first, second = summed[:, : 2 * HW], summed[:, 2 * HW :]
    mine = jnp.where(h == 0, first, second)
    other = jnp.where(h == 0, second, first)
    drow, dlane = iota((CH, 2 * HW), 0), iota((CH, 2 * HW), 1)

    def square_line(a):
        return a[LIVE_CH : LIVE_CH + 1] + a[LIVE_CH + 1 : LIVE_CH + 2]

    line = square_line(other)
    high = line.astype(BF16).astype(F32)
    ysend[...] = jnp.where(drow == LIVE_CH, high, jnp.where(drow == LIVE_CH + 1, line - high, other)).astype(BF16)
    across = remote(ysend, ybuf, partner)

    for copy in from_left[0] + from_right[0]:
        copy.wait_recv()
    far = [
        remote(feat.at[0, 3, TOP], feat.at[0, 2, TOP], right),
        remote(feat.at[0, 1, LOW], feat.at[0, 2, LOW], left),
    ]
    from_left.append({})
    from_right.append({})
    for p in (0, 2, 1, 3):
        crossed[p].wait_recv()
        from_left[1][p] = remote(feat.at[1, 0, PIECES[p]], feat.at[1, 3, PIECES[p]], right)
        from_right[1][p] = remote(feat.at[1, 0, PIECES[p]], feat.at[1, 1, PIECES[p]], left)

    across.wait_recv()
    summed = mine + ybuf[...].astype(F32)
    line = square_line(summed)
    squares = jnp.sum(jnp.where(drow == dlane, line, 0.0), axis=1, keepdims=True)
    scaled = summed * lax.rsqrt(squares / D + 1e-06)
    filled = iota((CH, HW), 0) < LIVE_CH
    keys = jnp.where(filled, rope(scaled[:, :HW], cos_k, sin_k), 0.0)
    values = jnp.where(filled, scaled[:, HW:], 0.0)
    kv[0, 0, 0] = jnp.concatenate([keys, values], axis=1).astype(BF16)

    y_moves = [remote(kv.at[0, 0, 0], kv.at[0, 0, NY - e], y_peers[e - 1]) for e in range(1, NY)]
    ups, downs = {}, {}

    def send_up(t, first, size):
        where = pl.ds(first, size)
        ups[t, first] = remote(kv.at[-t % NZ, 0, where], kv.at[(-t - 1) % NZ, 0, where], up)

    def send_down(t, first, size):
        where = pl.ds(first, size)
        downs[t, first] = remote(kv.at[t, 0, where], kv.at[t + 1, 0, where], down)

    send_up(0, 0, 1)
    send_down(0, 0, 1)

    fetches[5].wait()
    pick = iota((T, T), 1) == iota((T, T), 0)
    cos_q, sin_q = tables(pos_ref, inv_ref, pick)
    sums = [jnp.zeros((T, 2 * HW), F32), jnp.zeros((T, 1), F32)]

    def add(g, d):
        piece = ((h + g) % 2) * NX + (x + d) % NX
        wide = feat[g, d].astype(F32)
        sums[1] = sums[1] + jnp.sum(wide * wide, axis=1, keepdims=True)
        gained = (wide * gains[pl.ds(piece, 1)]).astype(BF16)
        sums[0] = sums[0] + jnp.dot(gained, qw[pl.ds(pl.multiple_of(piece * DS, DS), DS)], preferred_element_type=F32)

    add(0, 0)
    for e in (3, 1, 2):
        y_moves[e - 1].wait_recv()
        send_up(0, NY - e, 1)
        send_down(0, NY - e, 1)
    siblings = {0: remote(kv.at[0, 0], kv.at[0, 1], sibling)}

    def to_sibling(d):
        siblings[d] = remote(kv.at[d, 0], kv.at[d, 1], sibling)

    def z_step(t):
        for first in (0, 2):
            came = [0, 1] if first == 0 else [2, 3]
            for d in came if t == 1 else [first]:
                ups[t - 1, d].wait_recv()
            if t < 3 or first == 0:
                send_up(t, first, 2)
            for d in came if t == 1 else [first]:
                downs[t - 1, d].wait_recv()
            if t < 3 or first == 2:
                send_down(t, first, 2)
        to_sibling(NZ - t)
        to_sibling(t)

    add(1, 0)
    for p in (0, 1):
        from_left[1][p].wait_recv()
        far.append(remote(feat.at[1, 3, PIECES[p]], feat.at[1, 2, PIECES[p]], right))
        from_right[1][p + 2].wait_recv()
        far.append(remote(feat.at[1, 1, PIECES[p + 2]], feat.at[1, 2, PIECES[p + 2]], left))
    z_step(1)
    add(0, 3)
    add(0, 1)
    far[0].wait_recv()
    far[1].wait_recv()
    add(0, 2)
    for p in (2, 3):
        from_left[1][p].wait_recv()
        from_right[1][p - 2].wait_recv()
    add(1, 3)
    add(1, 1)
    z_step(2)
    for copy in far[2:]:
        copy.wait_recv()
    add(1, 2)
    queries = sums[0] * (lax.rsqrt(sums[1] / D + 1e-06) * QSCALE)
    for k in range(2):
        q_all[0, k] = rope(queries[:, k * HW : (k + 1) * HW], cos_q, sin_q).astype(BF16)
    q_moves = {NX - e: remote(q_all.at[0], q_all.at[NX - e], x_peers[e - 1]) for e in (1, 3, 2)}

    key = iota((T, CH), 1)
    own_counted = (key * NX + x <= iota((T, CH), 0)) & (key < LIVE_CH) & (key * NX + x < total)

    def with_ones(values):
        return jnp.concatenate([values, jnp.ones(values.shape, BF16)], axis=1)

    def begin(j):
        own = kv[0, 0, 0]
        for k in range(2):
            s = lax.dot_general(q_all[j, k], own[:, :HW], NT, preferred_element_type=F32)
            s = jnp.where(own_counted, s, MASKED)
            m = jnp.maximum(jnp.max(s, axis=1, keepdims=True), LEAST)
            m_ref[j, k] = m
            acc_ref[j, k] = jnp.dot(jnp.exp2(s - m).astype(BF16), with_ones(own[:, HW:]), preferred_element_type=F32)

    def attend(j, start, count):
        def one(n, carry):
            pair = (start + n) % (NZ // 2)
            block = jnp.concatenate([kv[pair * 2 + u].reshape(NC * NY * CH, 2 * HW) for u in range(2)], axis=0)
            keys, values = block[:, :HW], with_ones(block[:, HW:])
            mask = jnp.concatenate([bias[pl.ds(pair * 2, 1)], bias[pl.ds(pair * 2 + 1, 1)]], axis=1)
            scores = [lax.dot_general(q_all[j, k], keys, NT, preferred_element_type=F32) + mask for k in range(2)]
            for k in range(2):
                before = m_ref[j, k]
                m = jnp.maximum(before, jnp.max(scores[k], axis=1, keepdims=True))
                p = jnp.exp2(scores[k] - m).astype(BF16)
                m_ref[j, k] = m
                acc_ref[j, k] = acc_ref[j, k] * jnp.exp2(before - m) + jnp.dot(p, values, preferred_element_type=F32)
            return carry

        lax.fori_loop(0, count, one, 0)

    eye = iota((T, T), 0) == iota((T, T), 1)
    stat[...] = jnp.zeros_like(stat)

    def finish(j):
        for k in range(2):
            acc = acc_ref[j, k]
            weight = acc[:, HW : HW + 1]
            some = weight > 0.0
            safe = jnp.where(some, weight, 1.0)
            o_part[j, k] = (acc[:, :HW] / safe).astype(BF16)
            level = jnp.where(some, m_ref[j, k] + jnp.log2(safe), MASKED)
            stat[j, k, 0:1, :T] = jnp.sum(jnp.where(eye, level, 0.0), axis=0, keepdims=True)

    begin(0)
    z_step(3)
    for d in (0, 1, 7, 6):
        siblings[d].wait_recv()
    attend(0, 3, 2)
    for n, j in enumerate((1, 3, 2)):
        q_moves[j].wait_recv()
        begin(j)
        attend(j, 3, 2)
        if n == 0:
            ups[3, 0].wait_recv()
            downs[3, 2].wait_recv()
            to_sibling(4)
    for d in (2, 3, 5, 4):
        siblings[d].wait_recv()
    parts = {}
    for j in (2, 1, 3):
        attend(j, 1, 2)
        finish(j)
        parts[NX - j] = [
            remote(stat.at[j], sbuf.at[NX - j], x_peers[j - 1]), remote(o_part.at[j], obuf.at[NX - j], x_peers[j - 1])
        ]
    attend(0, 1, 2)
    finish(0)

    def column(line):
        return jnp.sum(jnp.where(eye, line[:, :T], 0.0), axis=1, keepdims=True)

    for j in (2, 3, 1):
        for copy in parts[j]:
            copy.wait_recv()
    live = iota((T, HW), 0) < total
    for k in range(2):
        levels = [stat[0, k][0:1]] + [sbuf[j, k][0:1] for j in range(1, NX)]
        peak = functools.reduce(jnp.maximum, levels)
        shares = [jnp.exp2(level - peak) for level in levels]
        whole_share = sum(shares)
        pieces = [o_part[0, k]] + [obuf[j, k] for j in range(1, NX)]
        summed = sum(column(s / whole_share) * a.astype(F32) for s, a in zip(shares, pieces))
        out_ref[0, :, k * HW : (k + 1) * HW] = jnp.where(live, summed, 0.0).astype(BF16)
    for copy in copies:
        copy.wait_send()


COPIES = 4 + 3 + 2 + 1 + 2 + 8 + 3 + 18 + 8 + 4 + 3 + 6


def whole():
    return pl.BlockSpec(memory_space=pltpu.VMEM)


def anywhere():
    return pl.BlockSpec(memory_space=pl.ANY)


def scalars():
    return pl.BlockSpec(memory_space=pltpu.SMEM)


LIMIT = 54 * 1024 * 1024


def per_device(
    vision_rows, audio_rows, vision_count, audio_count, position_ids, audio_proj, norm_gain, q_weight, key_value_weight
):
    lane = np.arange(HW) % (HW // 2)
    inverse = np.exp(-math.log(1000000.0) * 2.0 * lane / HW).astype(np.float32)[None]
    return pl.pallas_call(
        layer_kernel,
        out_shape=jax.ShapeDtypeStruct((1, T, 2 * HW), BF16),
        in_specs=[scalars(), scalars(), anywhere(), whole(), whole()] + [anywhere()] * 5,
        out_specs=whole(),
        scratch_shapes=[
            pltpu.VMEM((3, 1, T), jnp.int32),
            pltpu.VMEM((1, VC, DS), BF16),
            pltpu.VMEM((1, AC, AW), BF16),
            pltpu.VMEM((DS, AW), BF16),
            pltpu.VMEM((DS, 4 * HW), BF16),
            pltpu.VMEM((D, 2 * HW), BF16),
            pltpu.VMEM((T, DS), BF16),
            pltpu.VMEM((8, DS), F32),
            pltpu.VMEM((2, NX, T, DS), BF16),
            pltpu.VMEM((NX, CH, 4 * HW), BF16),
            pltpu.VMEM((NX, CH, 4 * HW), BF16),
            pltpu.VMEM((CH, 2 * HW), BF16),
            pltpu.VMEM((CH, 2 * HW), BF16),
            pltpu.VMEM((NX, 2, T, HW), BF16),
            pltpu.VMEM((NZ, NC, NY, CH, 2 * HW), BF16),
            pltpu.VMEM((NZ, NC * NY * CH), F32),
            pltpu.VMEM((NX, 2, T, 1), F32),
            pltpu.VMEM((NX, 2, T, 2 * HW), F32),
            pltpu.VMEM((NX, 2, T, HW), BF16),
            pltpu.VMEM((NX, 2, 8, 2 * HW), F32),
            pltpu.VMEM((NX, 2, T, HW), BF16),
            pltpu.VMEM((NX, 2, 8, 2 * HW), F32),
            pltpu.SemaphoreType.DMA((6,)),
            pltpu.SemaphoreType.DMA((COPIES,)),
            pltpu.SemaphoreType.DMA((COPIES,)),
        ],
        compiler_params=pltpu.CompilerParams(collective_id=0, has_side_effects=True, vmem_limit_bytes=LIMIT),
        name="layer",
    )(
        vision_count, audio_count, position_ids, jnp.asarray(inverse), norm_gain.reshape(D // HW, HW),
        vision_rows, audio_rows, audio_proj.T, key_value_weight, q_weight,
    )


def solution(mesh):
    placed = (
        P("ctx", None, "tp"),
        P("ctx", None, None),
        P(),
        P(),
        P(None, "ctx", None),
        P(None, "tp"),
        P(),
        P(None, "tp"),
        P("tp", None),
    )
    return jax.shard_map(
        per_device, mesh=mesh, in_specs=placed, out_specs=P("ctx", None, "tp"), check_vma=False
    )
```

```python
import functools
import math

import jax
import jax.numpy as jnp
import numpy as np
from jax import lax
from jax.experimental import pallas as pl
from jax.experimental.pallas import tpu as pltpu
from jax.sharding import PartitionSpec as P

HW = 128
MESH = pl.DeviceIdType.MESH
F32 = jnp.float32
BF16 = jnp.bfloat16

NY, NZ, NC, NX = 4, 8, 2, 4
VC, AC, T = 160, 64, 224
AW = 1280
DS, D = 448, 3584
CH = 64
LIVE_CH = T // NX
TOP, LOW = pl.ds(0, T // 2), pl.ds(T // 2, T // 2)
PIECES = [pl.ds(0, 64), pl.ds(64, 48), pl.ds(112, 64), pl.ds(176, 48)]
NT = (((1,), (1,)), ((), ()))
MASKED, LEAST = -1e30, -1e29
QSCALE = HW**-0.5 * math.log2(math.e)


def iota(shape, dim):
    return lax.broadcasted_iota(jnp.int32, shape, dim)


def place():
    ctx, tp = lax.axis_index("ctx"), lax.axis_index("tp")
    return dict(yl=ctx // (NZ * NC), z=(ctx // NC) % NZ, core=ctx % NC, h=tp // NX, x=tp % NX, ctx=ctx, tp=tp)


def device(at, yl=None, z=None, core=None, h=None, x=None):
    yl = at["yl"] if yl is None else yl
    z = at["z"] if z is None else z
    core = at["core"] if core is None else core
    h = at["h"] if h is None else h
    x = at["x"] if x is None else x
    return ((yl * NZ + z) * NC + core, h * NX + x)


def swap_halves(a):
    return jnp.concatenate([a[:, HW // 2 :], a[:, : HW // 2]], axis=1)


def rope(a, cos, sin):
    return a * cos + swap_halves(a) * sin


def tables(pos_ref, inv_ref, pick):
    rows = pick.shape[0]
    ids = [
        jnp.sum(jnp.where(pick, pos_ref[k].astype(F32), 0.0), axis=1, keepdims=True) for k in range(3)
    ]
    lane = iota((rows, HW), 1)
    freq = lane % (HW // 2)
    first = HW // 8
    second = (HW // 2 - first) // 2
    chosen = jnp.where(freq < first, ids[0], jnp.where(freq < first + second, ids[1], ids[2]))
    angle = chosen * inv_ref[...]
    sin = jnp.sin(angle)
    return jnp.cos(angle), jnp.where(lane < HW // 2, -sin, sin)


def gain_rows(gain_ref):
    g = gain_ref[...]
    half = HW // 2
    rows = []
    for u in range(4):
        r = [g[7 * u + k : 7 * u + k + 1] for k in range(7)]
        rows.append(jnp.concatenate([r[0], r[1], r[2], r[3][:, :half]], axis=1))
        rows.append(jnp.concatenate([r[3][:, half:], r[4], r[5], r[6]], axis=1))
    return jnp.concatenate(rows, axis=0)


def layer_kernel(
    vcount, acount, pos_hbm, inv_ref, gain_ref, vision_hbm, audio_hbm, proj_hbm, kvw_hbm, qw_hbm,
    out_ref,
    pos_ref, vision_ref, audio_ref, proj_ref, kvw_ref, qw,
    stacked, gains, feat, part, xbuf, ysend, ybuf, q_all, kv, bias, m_ref, acc_ref, o_part, stat, obuf, sbuf,
    fetch_sem, ssem, rsem,
):
    at = place()
    ctx, tp, x, h = at["ctx"], at["tp"], at["x"], at["h"]
    fetches = []
    for src, dst in [
        (audio_hbm, audio_ref), (proj_hbm, proj_ref), (vision_hbm, vision_ref), (kvw_hbm, kvw_ref), (pos_hbm, pos_ref), (qw_hbm, qw)
    ]:
        fetches.append(pltpu.make_async_copy(src, dst, fetch_sem.at[len(fetches)]))
        fetches[-1].start()

    right = device(at, x=(x + 1) % NX)
    left = device(at, x=(x + 3) % NX)
    up = device(at, z=(at["z"] + 1) % NZ)
    down = device(at, z=(at["z"] + 7) % NZ)
    sibling = device(at, core=1 - at["core"])
    partner = device(at, h=1 - h)
    x_peers = [device(at, x=(x + e) % NX) for e in range(1, NX)]
    y_peers = [device(at, yl=(at["yl"] + e) % NY) for e in range(1, NY)]
    greeted = [up, down, sibling, partner] + x_peers + y_peers
    barrier = pltpu.get_barrier_semaphore()
    for other in greeted:
        pl.semaphore_signal(barrier, inc=1, device_id=other, device_id_type=MESH)

    copies = []

    def remote(src, dst, to):
        i = len(copies)
        copy = pltpu.make_async_remote_copy(
            src_ref=src, dst_ref=dst, send_sem=ssem.at[i], recv_sem=rsem.at[i], device_id=to, device_id_type=MESH
        )
        copies.append(copy)
        copy.start()
        return copy

    vision_here = vcount[ctx]
    total = vision_here + acount[ctx]
    fetches[0].wait()
    fetches[1].wait()
    stacked[VC:] = lax.dot_general(audio_ref[0], proj_ref[...], NT, preferred_element_type=F32).astype(BF16)
    fetches[2].wait()
    stacked[:VC] = vision_ref[0]

    def picked(slot, valid):
        source = jnp.where(slot < vision_here, slot, VC + slot - vision_here)
        hit = (iota((slot.shape[0], T), 1) == source) & (slot < total) & valid
        onehot = jnp.where(hit, 1.0, 0.0).astype(BF16)
        return jnp.dot(onehot, stacked[...], preferred_element_type=F32)

    slot = iota((T, 1), 0)
    feat[0, 0] = picked(slot, slot >= 0).astype(BF16)

    row = iota((NX * CH, 1), 0)
    chunk_row = row % CH
    chunked = picked(chunk_row * NX + row // CH, chunk_row < LIVE_CH)
    squares = jnp.sum(chunked * chunked, axis=1, keepdims=True)
    gains[...] = gain_rows(gain_ref)
    gained = (chunked * gains[pl.ds(tp, 1)]).astype(BF16)
    fetches[3].wait()
    term = jnp.dot(gained, kvw_ref[...], preferred_element_type=F32)
    drow, dlane = iota((CH, 2 * HW), 0), iota((CH, 2 * HW), 1)
    for j in range(NX):
        rows = slice(j * CH, (j + 1) * CH)
        line = jnp.sum(jnp.where(drow == dlane, squares[rows], 0.0), axis=0, keepdims=True)
        high = line.astype(BF16).astype(F32)
        for g in range(2):
            block = jnp.concatenate(
                [term[rows, g * HW : (g + 1) * HW], term[rows, (2 + g) * HW : (3 + g) * HW]], axis=1
            )
            block = jnp.where(drow == LIVE_CH, high, jnp.where(drow == LIVE_CH + 1, line - high, block))
            part[j, g] = block.astype(BF16)
    pl.semaphore_wait(barrier, len(greeted))

    def send_terms(own):
        half = h if own else 1 - h
        return [remote(part.at[(x + e) % NX, half], xbuf.at[own, NX - e], x_peers[e - 1]) for e in (2, 1, 3)]

    terms = [send_terms(0)]
    crossed = {p: remote(feat.at[0, 0, PIECES[p]], feat.at[1, 0, PIECES[p]], partner) for p in range(4)}
    terms.append(send_terms(1))
    from_left = remote(feat.at[0, 0], feat.at[0, 3], right)
    from_right = remote(feat.at[0, 0], feat.at[0, 1], left)

    fetches[4].wait()
    pick = iota((CH, T), 1) == iota((CH, T), 0) * NX + x
    cos_k, sin_k = tables(pos_ref, inv_ref, pick)

    dz, lane = iota((NZ, NC * NY * CH), 0), iota((NZ, NC * NY * CH), 1)
    dc, dy, i = lane // (NY * CH), (lane // CH) % NY, lane % CH
    stretch = (((at["yl"] + dy) % NY) * NZ + (at["z"] + dz) % NZ) * NC + (at["core"] + dc) % NC
    lengths = jnp.zeros_like(stretch)
    for k in range(NY * NZ * NC):
        lengths = jnp.where(stretch == k, vcount[k] + acount[k], lengths)
    counted = (stretch < ctx) & (i < LIVE_CH) & (i * NX + x < lengths)
    bias[...] = jnp.where(counted, 0.0, MASKED)

    fetches[5].wait()
    pick = iota((T, T), 1) == iota((T, T), 0)
    cos_q, sin_q = tables(pos_ref, inv_ref, pick)
    sums, weights = {}, {}

    def add(half, g, d):
        rows = pl.ds(half * (T // 2), T // 2)
        piece = ((h + g) % 2) * NX + (x + d) % NX
        wide = feat[g, d, rows].astype(F32)
        square = jnp.sum(wide * wide, axis=1, keepdims=True)
        gained = (wide * gains[pl.ds(piece, 1)]).astype(BF16)
        term = jnp.dot(gained, qw[pl.ds(pl.multiple_of(piece * DS, DS), DS)], preferred_element_type=F32)
        sums[half] = sums[half] + term if half in sums else term
        weights[half] = weights[half] + square if half in weights else square

    q_moves = {}

    def send_queries(half):
        rows = slice(half * (T // 2), (half + 1) * (T // 2))
        where = pl.ds(half * (T // 2), T // 2)
        queries = sums[half] * (lax.rsqrt(weights[half] / D + 1e-06) * QSCALE)
        for k in range(2):
            q_all[0, k, where] = rope(queries[:, k * HW : (k + 1) * HW], cos_q[rows], sin_q[rows]).astype(BF16)
        for e in (2, 1, 3):
            q_moves[half, NX - e] = remote(q_all.at[0, :, where], q_all.at[NX - e, :, where], x_peers[e - 1])

    add(0, 0, 0)
    add(1, 0, 0)
    def add_terms(own):
        total_term = part[x, h if own else 1 - h].astype(F32)
        for copy, e in zip(terms[own], (2, 1, 3)):
            copy.wait_recv()
            total_term = total_term + xbuf[own, NX - e].astype(F32)
        return total_term

    def square_line(a):
        return a[LIVE_CH : LIVE_CH + 1] + a[LIVE_CH + 1 : LIVE_CH + 2]

    other = add_terms(0)
    line = square_line(other)
    high = line.astype(BF16).astype(F32)
    ysend[...] = jnp.where(drow == LIVE_CH, high, jnp.where(drow == LIVE_CH + 1, line - high, other)).astype(BF16)
    across = remote(ysend, ybuf, partner)
    mine = add_terms(1)

    from_left.wait_recv()
    from_right.wait_recv()
    far = [
        remote(feat.at[0, 3, TOP], feat.at[0, 2, TOP], right),
        remote(feat.at[0, 1, LOW], feat.at[0, 2, LOW], left),
    ]
    spread = {}
    for p in range(4):
        crossed[p].wait_recv()
        for e in (2, 1, 3):
            spread[p, NX - e] = remote(feat.at[1, 0, PIECES[p]], feat.at[1, NX - e, PIECES[p]], x_peers[e - 1])

    def land(half, d):
        spread[2 * half, d].wait_recv()
        spread[2 * half + 1, d].wait_recv()
        add(half, 1, d)

    across.wait_recv()
    summed = mine + ybuf[...].astype(F32)
    line = square_line(summed)
    squares = jnp.sum(jnp.where(drow == dlane, line, 0.0), axis=1, keepdims=True)
    scaled = summed * lax.rsqrt(squares / D + 1e-06)
    filled = iota((CH, HW), 0) < LIVE_CH
    keys = jnp.where(filled, rope(scaled[:, :HW], cos_k, sin_k), 0.0)
    values = jnp.where(filled, scaled[:, HW:], 0.0)
    kv[0, 0, 0] = jnp.concatenate([keys, values], axis=1).astype(BF16)

    y_moves = [remote(kv.at[0, 0, 0], kv.at[0, 0, NY - e], y_peers[e - 1]) for e in range(1, NY)]
    ups, downs = {}, {}

    def send_up(t, first, size):
        where = pl.ds(first, size)
        ups[t, first] = remote(kv.at[-t % NZ, 0, where], kv.at[(-t - 1) % NZ, 0, where], up)

    def send_down(t, first, size):
        where = pl.ds(first, size)
        downs[t, first] = remote(kv.at[t, 0, where], kv.at[t + 1, 0, where], down)

    send_up(0, 0, 1)
    send_down(0, 0, 1)

    for half in range(2):
        add(half, 0, 3)
        add(half, 0, 1)
        far[half].wait_recv()
        add(half, 0, 2)
    for e in (3, 1, 2):
        y_moves[e - 1].wait_recv()
        send_up(0, NY - e, 1)
        send_down(0, NY - e, 1)
    siblings = {0: remote(kv.at[0, 0], kv.at[0, 1], sibling)}

    def to_sibling(d):
        siblings[d] = remote(kv.at[d, 0], kv.at[d, 1], sibling)

    def z_step(t):
        for first in (0, 2):
            came = [0, 1] if first == 0 else [2, 3]
            for d in came if t == 1 else [first]:
                ups[t - 1, d].wait_recv()
            if t < 3 or first == 0:
                send_up(t, first, 2)
            for d in came if t == 1 else [first]:
                downs[t - 1, d].wait_recv()
            if t < 3 or first == 2:
                send_down(t, first, 2)
        to_sibling(NZ - t)
        to_sibling(t)

    add(0, 1, 0)
    add(1, 1, 0)
    for d in (1, 3, 2):
        land(0, d)
    send_queries(0)
    z_step(1)
    for d in (1, 3, 2):
        land(1, d)
    send_queries(1)
    z_step(2)

    key = iota((T, CH), 1)
    own_counted = (key * NX + x <= iota((T, CH), 0)) & (key < LIVE_CH) & (key * NX + x < total)

    def with_ones(values):
        return jnp.concatenate([values, jnp.ones(values.shape, BF16)], axis=1)

    def begin(j):
        own = kv[0, 0, 0]
        for k in range(2):
            s = lax.dot_general(q_all[j, k], own[:, :HW], NT, preferred_element_type=F32)
            s = jnp.where(own_counted, s, MASKED)
            m = jnp.maximum(jnp.max(s, axis=1, keepdims=True), LEAST)
            m_ref[j, k] = m
            acc_ref[j, k] = jnp.dot(jnp.exp2(s - m).astype(BF16), with_ones(own[:, HW:]), preferred_element_type=F32)

    def attend(blocks, start, count, width=1):
        def one(n, carry):
            block = jnp.concatenate([kv[d].reshape(NC * NY * CH, 2 * HW) for d in blocks], axis=0)
            keys, values = block[:, :HW], with_ones(block[:, HW:])
            mask = jnp.concatenate([bias[d : d + 1] for d in blocks], axis=1)
            heads = [(start + n * width + u, k) for u in range(width) for k in range(2)]

            def score(j, k):
                return lax.dot_general(q_all[j, k], keys, NT, preferred_element_type=F32) + mask

            ahead = [score(*heads[0]), score(*heads[1])]
            for i, (j, k) in enumerate(heads):
                scores = ahead.pop(0)
                if i + 2 < len(heads):
                    ahead.append(score(*heads[i + 2]))
                before = m_ref[j, k]
                m = jnp.maximum(before, jnp.max(scores, axis=1, keepdims=True))
                p = jnp.exp2(scores - m).astype(BF16)
                m_ref[j, k] = m
                acc_ref[j, k] = acc_ref[j, k] * jnp.exp2(before - m) + jnp.dot(p, values, preferred_element_type=F32)
            return carry

        if count == width:
            one(0, 0)
        else:
            lax.fori_loop(0, count // width, one, 0)

    eye = iota((T, T), 0) == iota((T, T), 1)
    stat[...] = jnp.zeros_like(stat)

    def finish(j):
        for k in range(2):
            acc = acc_ref[j, k]
            weight = acc[:, HW : HW + 1]
            some = weight > 0.0
            safe = jnp.where(some, weight, 1.0)
            o_part[j, k] = (acc[:, :HW] / safe).astype(BF16)
            level = jnp.where(some, m_ref[j, k] + jnp.log2(safe), MASKED)
            stat[j, k : k + 1, :T] = jnp.sum(jnp.where(eye, level, 0.0), axis=0, keepdims=True)

    begin(0)
    siblings[0].wait_recv()
    siblings[1].wait_recv()
    attend((0, 1), 0, 1)
    for j in (1, 3, 2):
        q_moves[0, j].wait_recv()
        q_moves[1, j].wait_recv()
        begin(j)
    attend((0, 1), 1, 3, 3)
    z_step(3)
    siblings[7].wait_recv()
    siblings[6].wait_recv()
    attend((7, 6), 0, 4, 4)
    ups[3, 0].wait_recv()
    downs[3, 2].wait_recv()
    to_sibling(4)
    for d in (2, 3, 5):
        siblings[d].wait_recv()
    attend((2, 3, 5), 1, 3, 3)
    siblings[4].wait_recv()
    parts = {}
    for j in (2, 1, 3):
        attend((4,), j, 1)
        finish(j)
        parts[NX - j] = [
            remote(stat.at[j], sbuf.at[NX - j], x_peers[j - 1]), remote(o_part.at[j], obuf.at[NX - j], x_peers[j - 1])
        ]
    attend((2, 3, 5, 4), 0, 1)
    finish(0)

    def column(line):
        return jnp.sum(jnp.where(eye, line[:, :T], 0.0), axis=1, keepdims=True)

    for j in (2, 3, 1):
        for copy in parts[j]:
            copy.wait_recv()
    live = iota((T, HW), 0) < total
    for k in range(2):
        levels = [stat[0, k : k + 1]] + [sbuf[j, k : k + 1] for j in range(1, NX)]
        peak = functools.reduce(jnp.maximum, levels)
        shares = [jnp.exp2(level - peak) for level in levels]
        whole_share = sum(shares)
        pieces = [o_part[0, k]] + [obuf[j, k] for j in range(1, NX)]
        summed = sum(column(s / whole_share) * a.astype(F32) for s, a in zip(shares, pieces))
        out_ref[0, :, k * HW : (k + 1) * HW] = jnp.where(live, summed, 0.0).astype(BF16)
    for copy in copies:
        copy.wait_send()


COPIES = 4 + 6 + 2 + 1 + 2 + 12 + 3 + 18 + 8 + 6 + 6


def whole():
    return pl.BlockSpec(memory_space=pltpu.VMEM)


def anywhere():
    return pl.BlockSpec(memory_space=pl.ANY)


def scalars():
    return pl.BlockSpec(memory_space=pltpu.SMEM)


LIMIT = 54 * 1024 * 1024


def per_device(
    vision_rows, audio_rows, vision_count, audio_count, position_ids, audio_proj, norm_gain, q_weight, key_value_weight
):
    lane = np.arange(HW) % (HW // 2)
    inverse = np.exp(-math.log(1000000.0) * 2.0 * lane / HW).astype(np.float32)[None]
    return pl.pallas_call(
        layer_kernel,
        out_shape=jax.ShapeDtypeStruct((1, T, 2 * HW), BF16),
        in_specs=[scalars(), scalars(), anywhere(), whole(), whole()] + [anywhere()] * 5,
        out_specs=whole(),
        scratch_shapes=[
            pltpu.VMEM((3, 1, T), jnp.int32),
            pltpu.VMEM((1, VC, DS), BF16),
            pltpu.VMEM((1, AC, AW), BF16),
            pltpu.VMEM((DS, AW), BF16),
            pltpu.VMEM((DS, 4 * HW), BF16),
            pltpu.VMEM((D, 2 * HW), BF16),
            pltpu.VMEM((T, DS), BF16),
            pltpu.VMEM((8, DS), F32),
            pltpu.VMEM((2, NX, T, DS), BF16),
            pltpu.VMEM((NX, 2, CH, 2 * HW), BF16),
            pltpu.VMEM((2, NX, CH, 2 * HW), BF16),
            pltpu.VMEM((CH, 2 * HW), BF16),
            pltpu.VMEM((CH, 2 * HW), BF16),
            pltpu.VMEM((NX, 2, T, HW), BF16),
            pltpu.VMEM((NZ, NC, NY, CH, 2 * HW), BF16),
            pltpu.VMEM((NZ, NC * NY * CH), F32),
            pltpu.VMEM((NX, 2, T, 1), F32),
            pltpu.VMEM((NX, 2, T, 2 * HW), F32),
            pltpu.VMEM((NX, 2, T, HW), BF16),
            pltpu.VMEM((NX, 8, 2 * HW), F32),
            pltpu.VMEM((NX, 2, T, HW), BF16),
            pltpu.VMEM((NX, 8, 2 * HW), F32),
            pltpu.SemaphoreType.DMA((6,)),
            pltpu.SemaphoreType.DMA((COPIES,)),
            pltpu.SemaphoreType.DMA((COPIES,)),
        ],
        compiler_params=pltpu.CompilerParams(collective_id=0, has_side_effects=True, vmem_limit_bytes=LIMIT),
        name="layer",
    )(
        vision_count, audio_count, position_ids, jnp.asarray(inverse), norm_gain.reshape(D // HW, HW),
        vision_rows, audio_rows, audio_proj.T, key_value_weight, q_weight,
    )


def solution(mesh):
    placed = (
        P("ctx", None, "tp"),
        P("ctx", None, None),
        P(),
        P(),
        P(None, "ctx", None),
        P(None, "tp"),
        P(),
        P(None, "tp"),
        P("tp", None),
    )
    return jax.shard_map(
        per_device, mesh=mesh, in_specs=placed, out_specs=P("ctx", None, "tp"), check_vma=False
    )
```
